256 devices in a mesh: grp: 8 (over z_lo, core), dev: 32 (over y, z_hi, x).
Axes of the slice: x: 4, y: 4, z: 8 (z_hi: 2, z_lo: 4; z = z_hi * 4 + z_lo), core: 2. Of those that a mesh axis runs over, the one named last changes fastest.
Arguments:
- voltages: bfloat16 [2048, 268288], P(('grp', 'dev')), may hold values from -6 to 6
- weights: bfloat16 [512, 2, 512, 2048], P('dev', None, None, 'grp'), may hold values from -0.125 to 0.125
- input_map: int32 [2048], P('grp'), may hold values from 0 to 255, as said below
- beam_order: int32 [512], replicated, may hold values from 0 to 511, each once
Outputs:
- beam_power: float32 [512, 16, 512], P('dev', None, 'grp')
The draws below stay inside these ranges and needn't reach their ends.
Inputs may be any that keep to these rules, and one draw needn't show every extreme that they name: `input_map`: each aligned block of 256 entries holds every number below 256 once. `beam_order`: each beam appears once.
All inputs are finite; a program needn't handle non-finite values.
Results may differ from the reference program's by a relative error of at most 0.0022.
Values may be sent and summed in bfloat16 or wider, within the bound.
No kernel may reach another device: no remote copies, remote signals or barrier semaphores. Data moves between devices by JAX's collectives and lax.ppermute only.
A program may use at most 128 MiB of HBM per device.

```python
import math
import jax
import jax.numpy as jnp
from jax import lax

INPUTS = 2048
CHAN = 1024
BEAMS = 512
TAPS = 4
UPCH = 16
WIN = 512
SPECTRA = 128
BAND_LO = 256
GROUP_INPUTS = 256
SAMPLES = 268288


def draw_input_map(key, part):
    key = jax.random.fold_in(key, 11)
    groups = INPUTS // GROUP_INPUTS
    keys = jax.random.split(key, groups)
    perms = jax.vmap(lambda one_key: jax.random.permutation(one_key, GROUP_INPUTS))(keys)
    return perms.reshape(-1).astype(jnp.int32)


def raised(entries, rng, source, target, blocks, factor):
    owner, partner = [(jnp.arange(entries.shape[position]) // (entries.shape[position] // blocks)).reshape([-1 if axis == position else 1 for axis in range(entries.ndim)]) for position in (source, target)]
    chosen = jax.random.permutation(rng, blocks)[partner]
    strong = (owner == chosen) | (owner == (partner + blocks // 2) % blocks)
    return jnp.where(strong, factor * entries, entries)


def block_levels(key, extent, shards, smallest, high):
    def one(axis_at, parts):
        heights = jax.random.uniform(jax.random.fold_in(jax.random.fold_in(key, 6), axis_at), (parts,), jnp.float32, smallest / len(shards), high / len(shards))
        return jnp.repeat(jnp.exp(heights), extent[axis_at] // parts).reshape((-1,) + (1,) * (len(extent) - axis_at - 1))

    gain = one(*shards[0])
    for cut in shards[1:]:
        gain = gain * one(*cut)
    return gain


def scatter_about(rng, extent, width, most, cuts=(), kind=jnp.bfloat16):
    result = jax.random.normal(rng, extent, jnp.float32) * width
    if len(cuts) > 0:
        result = block_levels(rng, extent, cuts, -0.22, 0.18) * result
    return jnp.clip(result, min=-most, max=most).astype(kind)


def heavy_noise(own_key, extent, spread, most, cuts, heavy, held_as=jnp.bfloat16):
    entries = spread * jax.random.normal(own_key, extent, jnp.float32)
    if cuts:
        entries = entries * block_levels(own_key, extent, cuts, -0.22, 0.18)
    return jnp.clip(raised(entries, jax.random.fold_in(own_key, 3), *heavy), -most, most).astype(held_as)


def setup_inputs(seed: int = 0) -> dict:
    key_of = jax.random.split(jax.random.key(seed), 5)
    voltages = scatter_about(key_of[0], (INPUTS, SAMPLES), 1.0, 6.0, ((0, 256),))
    weights = heavy_noise(key_of[1], (WIN, 2, BEAMS, INPUTS), (2 * INPUTS) ** -0.5, 0.125, ((0, 32), (3, 8)), (3, 2, 8, 2.0))
    input_map = draw_input_map(jax.random.fold_in(key_of[4], 71), 0)
    beam_order = jax.random.permutation(key_of[3], BEAMS).astype(jnp.int32)
    return dict(voltages=voltages, weights=weights, input_map=input_map, beam_order=beam_order)


def taper_table(nfft, tap_count):
    index = jnp.arange(tap_count * nfft, dtype=jnp.float32)
    centred = (index - tap_count * nfft / 2.0 + 0.5) / nfft
    window = 0.5 - 0.5 * jnp.cos(2.0 * math.pi * (index + 0.5) / (tap_count * nfft))
    return (jnp.sinc(centred) * window).reshape(tap_count, nfft)

def transform_table(chan, first, count):
    nfft = 2 * chan
    sample_ids = jnp.arange(nfft, dtype=jnp.int32)
    chan_ids = first + jnp.arange(count, dtype=jnp.int32)
    phases = chan_ids[:, None] * sample_ids[None, :] % nfft
    angles = 2.0 * math.pi * phases.astype(jnp.float32) / nfft
    factor = 1.0 / math.sqrt(chan)
    stacked = jnp.stack([jnp.cos(angles) * factor, -jnp.sin(angles) * factor], axis=1)
    return stacked.reshape(2 * count, nfft).astype(jnp.bfloat16)

def channelize(volts, chan, first, count, tap_count, spectra):
    nfft = 2 * chan
    frames = volts.astype(jnp.float32).reshape(volts.shape[0], spectra + tap_count - 1, nfft)
    taper = taper_table(nfft, tap_count)
    summed = taper[0] * frames[:, 0:spectra, :]
    for tap_index in range(1, tap_count):
        summed = summed + taper[tap_index] * frames[:, tap_index:tap_index + spectra, :]
    summed = summed.astype(jnp.bfloat16)
    return jnp.einsum('kn,isn->ksi', transform_table(chan, first, count), summed, preferred_element_type=jnp.float32).astype(jnp.bfloat16)

def detect(beams, upch):
    blocks = beams.shape[3] // upch
    split_beams = beams.reshape(beams.shape[0], beams.shape[1], 2, blocks, upch)
    sub_ids = jnp.arange(upch, dtype=jnp.int32)
    phases = sub_ids[:, None] * sub_ids[None, :] % upch
    angles = 2.0 * math.pi * phases.astype(jnp.float32) / upch
    real_table = jnp.cos(angles) / math.sqrt(upch)
    imag_table = -jnp.sin(angles) / math.sqrt(upch)
    real_in = split_beams[:, :, 0]
    imag_in = split_beams[:, :, 1]
    highest = lax.Precision.HIGHEST
    real_out = jnp.einsum('ut,bckt->bcku', real_table, real_in, precision=highest) - jnp.einsum('ut,bckt->bcku', imag_table, imag_in, precision=highest)
    imag_out = jnp.einsum('ut,bckt->bcku', real_table, imag_in, precision=highest) + jnp.einsum('ut,bckt->bcku', imag_table, real_in, precision=highest)
    power = lax.optimization_barrier(jnp.mean(real_out * real_out + imag_out * imag_out, axis=2))
    return jnp.transpose(power, (1, 2, 0))

def reference(voltages, weights, input_map, beam_order):
    groups = INPUTS // GROUP_INPUTS
    grouped = voltages.reshape(groups, GROUP_INPUTS, SAMPLES)
    spectra_all = lax.map(lambda volts: channelize(volts, CHAN, BAND_LO, WIN, TAPS, SPECTRA), grouped)
    spectra_all = jnp.transpose(spectra_all, (1, 2, 0, 3)).reshape(WIN, 2, SPECTRA, INPUTS)
    input_ids = jnp.arange(INPUTS, dtype=jnp.int32)
    feeds = input_ids // GROUP_INPUTS * GROUP_INPUTS + input_map
    inverse = jnp.zeros((INPUTS,), jnp.int32).at[feeds].set(input_ids)
    feed_data = jnp.take(spectra_all, inverse, axis=3)

    def one_channel(pair):
        chan_weights, chan_data = pair
        wide_weights = chan_weights.astype(jnp.float32)
        wide_data = chan_data.astype(jnp.float32)
        product = jnp.einsum('pbi,qsi->bpqs', wide_weights, wide_data, precision=lax.Precision.HIGHEST)
        real_part = product[:, 0, 0] - product[:, 1, 1]
        imag_part = product[:, 0, 1] + product[:, 1, 0]
        beams = jnp.stack([real_part, imag_part], axis=1)
        beams = jnp.take(beams, beam_order, axis=0)
        return detect(beams[:, None], UPCH)[0]
    return lax.map(one_channel, (weights, feed_data))
```

```python
import math

import jax
import jax.numpy as jnp
import numpy as np
from jax import lax
from jax.experimental import pallas as pl
from jax.experimental.pallas import tpu as pltpu
from jax.sharding import Mesh
from jax.sharding import PartitionSpec as P

CHAN = 1024
NFFT = 2048
TAPS = 4
UPCH = 16
WIN = 512
SPECTRA = 128
BAND_LO = 256
LANES = 128
OWN = 8
NT = NFFT // LANES
MIB = 1 << 20


def taper_table():
    index = np.arange(TAPS * NFFT, dtype=np.float64)
    centred = (index - TAPS * NFFT / 2.0 + 0.5) / NFFT
    window = 0.5 - 0.5 * np.cos(2.0 * math.pi * (index + 0.5) / (TAPS * NFFT))
    return (np.sinc(centred) * window).astype(np.float32).reshape(TAPS, NFFT)


def transform_table():
    chan_ids = BAND_LO + np.arange(WIN)
    angles = 2.0 * math.pi * ((chan_ids[:, None] * np.arange(NFFT)[None, :]) % NFFT) / NFFT
    stacked = np.stack([np.cos(angles), -np.sin(angles)], axis=1) / math.sqrt(CHAN)
    return stacked.reshape(2 * WIN, NFFT).astype(jnp.bfloat16)


def channelize_kernel(volts_ref, taper_ref, table_ref, out_ref, fir_ref, frames_ref, turn_ref):
    def fir_tile(nt, _):
        lane = pl.multiple_of(nt * LANES, LANES)
        taps = [taper_ref[t, :, pl.ds(lane, LANES)] for t in range(TAPS)]

        def load(frame):
            at = pl.multiple_of(frame * NFFT + lane, LANES)
            return volts_ref[:, pl.ds(at, LANES)].astype(jnp.float32)

        def spectra(s0, held):
            held = list(held)
            for k in range(16):
                s = s0 * 16 + k
                held.append(load(s + TAPS - 1))
                total = taps[0] * held[0]
                for t in range(1, TAPS):
                    total = total + taps[t] * held[t]
                held = held[1:]
                fir_ref[pl.ds(pl.multiple_of(s * OWN, OWN), OWN), :] = total
            return tuple(held)

        lax.fori_loop(0, SPECTRA // 16, spectra, tuple(load(t) for t in range(TAPS - 1)))
        for i in range(OWN):
            frames_ref[pl.ds(i * SPECTRA, SPECTRA), pl.ds(lane, LANES)] = fir_ref[
                pl.ds(i, SPECTRA, stride=OWN), :
            ].astype(jnp.bfloat16)
        return 0

    lax.fori_loop(0, NT, fir_tile, 0)
    rows = 256

    def transform(block, _):
        at = pl.multiple_of(block * rows, rows)
        table = table_ref[pl.ds(at, rows), :]
        for pair in range(OWN // 2):
            part = lax.dot_general(
                table,
                frames_ref[pl.ds(pair * 2 * SPECTRA, 2 * SPECTRA), :],
                (((1,), (1,)), ((), ())),
                preferred_element_type=jnp.float32,
            )
            for half in range(2):
                turn_ref[pl.ds(pair * 2 + half, rows, stride=OWN), :] = part[
                    :, half * SPECTRA : (half + 1) * SPECTRA
                ]
        out_ref[pl.ds(pl.multiple_of(at * OWN, rows * OWN), rows * OWN), :] = turn_ref[...].astype(jnp.bfloat16)
        return 0

    lax.fori_loop(0, 2 * WIN // rows, transform, 0)


def channelize(volts):
    taper = jnp.asarray(np.broadcast_to(taper_table()[:, None, :], (TAPS, OWN, NFFT)).copy())
    table = jnp.asarray(transform_table())
    return pl.pallas_call(
        channelize_kernel,
        out_shape=jax.ShapeDtypeStruct((2 * WIN * OWN, SPECTRA), jnp.bfloat16),
        scratch_shapes=[
            pltpu.VMEM((SPECTRA * OWN, LANES), jnp.float32),
            pltpu.VMEM((SPECTRA * OWN, NFFT), jnp.bfloat16),
            pltpu.VMEM((256 * OWN, SPECTRA), jnp.float32),
        ],
        compiler_params=pltpu.CompilerParams(vmem_limit_bytes=48 * MIB),
    )(volts, taper, table)


def weight_kernel(order_ref, map_ref, weights_ref, out_ref, pick_ref, place_ref):
    beams = weights_ref.shape[2]
    feeds = weights_ref.shape[3]

    @pl.when(pl.program_id(0) == 0)
    def _():
        ids = lax.broadcasted_iota(jnp.int32, (beams, beams), 1)
        pick_ref[...] = jnp.where(order_ref[...] == ids, 1.0, 0.0).astype(jnp.bfloat16)
        feed = lax.broadcasted_iota(jnp.int32, (feeds, 2 * feeds), 0)
        part = (lax.broadcasted_iota(jnp.int32, (feeds, 2 * feeds), 1) // OWN) % 2
        match = jnp.where(map_ref[...] == feed, 1.0, 0.0)
        of_real = jnp.where(part == 0, match, 0.0).astype(jnp.bfloat16)
        of_imag = jnp.where(part == 1, match, 0.0).astype(jnp.bfloat16)
        place_ref[0:feeds, 0 : 2 * feeds] = of_real
        place_ref[feeds:, 0 : 2 * feeds] = -of_imag
        place_ref[0:feeds, 2 * feeds :] = of_imag
        place_ref[feeds:, 2 * feeds :] = of_real

    wide = jnp.concatenate([weights_ref[0, 0], weights_ref[0, 1]], axis=1)
    picked = jnp.dot(pick_ref[...], wide, preferred_element_type=jnp.float32).astype(jnp.bfloat16)
    out_ref[0] = jnp.dot(picked, place_ref[...], preferred_element_type=jnp.float32).astype(jnp.bfloat16)


def arrange_weights(weights, order, inputs_map):
    chans, _, beams, feeds = weights.shape
    spread = jnp.broadcast_to(inputs_map.reshape(-1, 1, OWN), (feeds // OWN, 2, OWN)).reshape(1, 2 * feeds)
    return pl.pallas_call(
        weight_kernel,
        grid=(chans,),
        out_shape=jax.ShapeDtypeStruct((chans, beams, 4 * feeds), jnp.bfloat16),
        in_specs=[
            pl.BlockSpec((beams, 1), lambda c: (0, 0)),
            pl.BlockSpec((1, 2 * feeds), lambda c: (0, 0)),
            pl.BlockSpec((1, 2, beams, feeds), lambda c: (c, 0, 0, 0)),
        ],
        out_specs=pl.BlockSpec((1, beams, 4 * feeds), lambda c: (c, 0, 0)),
        scratch_shapes=[
            pltpu.VMEM((beams, beams), jnp.bfloat16),
            pltpu.VMEM((2 * feeds, 4 * feeds), jnp.bfloat16),
        ],
        compiler_params=pltpu.CompilerParams(vmem_limit_bytes=32 * MIB),
        cost_estimate=pl.CostEstimate(
            flops=2 * chans * beams * 2 * feeds * (beams + 4 * feeds),
            bytes_accessed=3 * 2 * weights.size,
            transcendentals=0,
        ),
    )(order.reshape(beams, 1), spread, weights)


def combine_kernel(weights_ref, data_ref, keep_ref, send_ref):
    beams, wide = weights_ref.shape[1:]
    spectra = data_ref.shape[3]
    half = beams // 2
    data = data_ref[:, 0].reshape(wide // 2, spectra)
    for part in range(2):
        product = jnp.dot(
            weights_ref[0, :, part * (wide // 2) : (part + 1) * (wide // 2)],
            data,
            preferred_element_type=jnp.float32,
        )
        keep_ref[:, 0, part] = product[:half].reshape(4, half // 4, spectra)
        send_ref[:, 0, part] = product[half:].reshape(4, half // 4, spectra).astype(jnp.bfloat16)


def combine(arranged, data):
    chans, beams, wide = arranged.shape
    sources, _, rows, spectra = data.shape
    shape = (4, chans, 2, beams // 8, spectra)
    block = pl.BlockSpec((4, 1, 2, beams // 8, spectra), lambda c: (0, c, 0, 0, 0))
    return pl.pallas_call(
        combine_kernel,
        grid=(chans,),
        out_shape=(jax.ShapeDtypeStruct(shape, jnp.float32), jax.ShapeDtypeStruct(shape, jnp.bfloat16)),
        in_specs=[
            pl.BlockSpec((1, beams, wide), lambda c: (c, 0, 0)),
            pl.BlockSpec((sources, 1, rows, spectra), lambda c: (0, c, 0, 0)),
        ],
        out_specs=(block, block),
        compiler_params=pltpu.CompilerParams(vmem_limit_bytes=32 * MIB),
    )(arranged, data)


def fine_tables():
    steps = np.arange(UPCH)
    angles = 2.0 * math.pi * (np.outer(steps, steps) % UPCH) / UPCH
    eye = np.eye(SPECTRA // UPCH)
    real = np.kron(eye, np.cos(angles) / math.sqrt(UPCH))
    imag = np.kron(eye, -np.sin(angles) / math.sqrt(UPCH))
    turn = np.block([[real, imag], [-imag, real]]).astype(np.float32)
    mean = np.tile(np.eye(UPCH) * UPCH / SPECTRA, (1, SPECTRA // UPCH)).astype(np.float32)
    return turn, mean


def detect_kernel(keep_ref, come_ref, turn_ref, mean_ref, out_ref):
    chans, _, beams, spectra = keep_ref.shape
    total = keep_ref[...] + come_ref[...].astype(jnp.float32)
    both = jnp.concatenate(
        [total[:, 0].reshape(chans * beams, spectra), total[:, 1].reshape(chans * beams, spectra)], axis=1
    )
    sub = jnp.dot(both, turn_ref[...], preferred_element_type=jnp.float32, precision=lax.Precision.HIGHEST)
    power = sub[:, :spectra] * sub[:, :spectra] + sub[:, spectra:] * sub[:, spectra:]
    mean = lax.dot_general(
        mean_ref[...],
        power,
        (((1,), (1,)), ((), ())),
        preferred_element_type=jnp.float32,
        precision=lax.Precision.HIGHEST,
    )
    for chan in range(chans):
        out_ref[chan] = mean[:, chan * beams : (chan + 1) * beams]


def detect(keep, come):
    chans, _, beams, _ = keep.shape
    turn, mean = fine_tables()
    return pl.pallas_call(
        detect_kernel,
        out_shape=jax.ShapeDtypeStruct((chans, UPCH, beams), jnp.float32),
        compiler_params=pltpu.CompilerParams(vmem_limit_bytes=32 * MIB),
    )(keep, come, jnp.asarray(turn), jnp.asarray(mean))


def swap(value, axis, distance, size):
    return lax.ppermute(value, axis, [(k, k ^ distance) for k in range(size)])


def on_device(voltages, weights, input_map, beam_order):
    chans = weights.shape[0]
    spectrum = channelize(voltages)
    devices = 2 * WIN // (2 * chans)
    turned = lax.all_to_all(
        spectrum.reshape(devices, chans * 2 * OWN, SPECTRA), ("y", "zh", "x"), split_axis=0, concat_axis=0, tiled=True
    )
    core, z = lax.axis_index("core"), lax.axis_index("zl")
    blocks = beam_order.reshape(4, 2, -1)
    near = jnp.where(core == 0, blocks, blocks[:, ::-1])
    near = jnp.where(z % 2 == 0, near, near.reshape(2, 2, 2, -1)[:, ::-1].reshape(near.shape))
    near = jnp.where(z // 2 == 0, near, near.reshape(2, 2, 2, -1)[::-1].reshape(near.shape))
    order = jnp.transpose(near, (1, 0, 2)).reshape(-1)
    arranged = arrange_weights(weights, order, input_map)
    keep, send = combine(arranged, turned.reshape(devices, chans, 2 * OWN, SPECTRA))
    total = keep + swap(send, "core", 1, 2).astype(jnp.float32)
    total = total.reshape((2, 2) + total.shape[1:])
    half = chans // 2
    first, second = total[:, :, :half], total[:, :, half:]
    first_in = swap(first[:, 1].astype(jnp.bfloat16), "zl", 1, 4)
    second_in = swap(second[1].astype(jnp.bfloat16), "zl", 2, 4)
    first = first[:, 0] + first_in.astype(jnp.float32)
    second = second[0] + second_in.astype(jnp.float32)
    first_in = swap(first[1].astype(jnp.bfloat16), "zl", 2, 4)
    second_in = swap(second[1].astype(jnp.bfloat16), "zl", 1, 4)
    return jnp.concatenate([detect(first[0], first_in), detect(second[0], second_in)], axis=0)


def solution(mesh):
    fine = Mesh(mesh.devices.reshape(4, 2, 4, 2, 4), ("zl", "core", "y", "zh", "x"))
    grp, dev = ("zl", "core"), ("y", "zh", "x")
    placed = (P(grp + dev, None), P(dev, None, None, grp), P(grp), P())
    return jax.shard_map(on_device, mesh=fine, in_specs=placed, out_specs=P(dev, None, grp), check_vma=False)
```

```python
import functools
import math

import jax
import jax.numpy as jnp
import numpy as np
from jax import lax
from jax.experimental import pallas as pl
from jax.experimental.pallas import tpu as pltpu
from jax.sharding import Mesh
from jax.sharding import PartitionSpec as P

CHAN = 1024
NFFT = 2048
TAPS = 4
UPCH = 16
WIN = 512
SPECTRA = 128
BAND_LO = 256
LANES = 128
OWN = 8
NT = NFFT // LANES
LARGE, SMALL = 60 << 20, 16 << 20
SHORT = pl.CostEstimate(flops=1, bytes_accessed=1, transcendentals=0)


def taper_table():
    index = np.arange(TAPS * NFFT, dtype=np.float64)
    centred = (index - TAPS * NFFT / 2.0 + 0.5) / NFFT
    window = 0.5 - 0.5 * np.cos(2.0 * math.pi * (index + 0.5) / (TAPS * NFFT))
    return (np.sinc(centred) * window).astype(np.float32).reshape(TAPS, NFFT)


def transform_table():
    chan_ids = BAND_LO + np.arange(WIN)
    angles = 2.0 * math.pi * ((chan_ids[:, None] * np.arange(NFFT)[None, :]) % NFFT) / NFFT
    stacked = np.stack([np.cos(angles), -np.sin(angles)], axis=1) / math.sqrt(CHAN)
    return stacked.reshape(2 * WIN, NFFT).astype(jnp.bfloat16)


FIR_BLOCK = 32
HALO = TAPS - 1


def transform_block(table, frames_ref, turn_ref):
    rows = table.shape[0]
    for pair in range(OWN // 2):
        part = lax.dot_general(
            table,
            frames_ref[pl.ds(pair * 2 * SPECTRA, 2 * SPECTRA), :],
            (((1,), (1,)), ((), ())),
            preferred_element_type=jnp.float32,
        )
        for half in range(2):
            turn_ref[pl.ds(pair * 2 + half, rows, stride=OWN), :] = part[:, half * SPECTRA : (half + 1) * SPECTRA]


PLANE = 16


def place(turn_ref, out_ref, mine):
    rows = turn_ref.shape[0] // PLANE
    for owner in range(PLANE):
        out_ref[mine ^ owner] = turn_ref[owner * rows : (owner + 1) * rows, :].astype(jnp.bfloat16)


def channelize_kernel(
    where_ref, volts_hbm, taper_ref, table_hbm, first_hbm, rest_hbm,
    volts_ref, table_ref, frames_ref, turn_ref, first_ref, rest_ref, sems,
):
    blocks = SPECTRA // FIR_BLOCK
    copies = []
    for block in range(blocks):
        first = block * FIR_BLOCK + (HALO if block else 0)
        last = (block + 1) * FIR_BLOCK + HALO
        span = pl.ds(first * NFFT, (last - first) * NFFT)
        copies.append(pltpu.make_async_copy(volts_hbm.at[:, span], volts_ref.at[:, span], sems.at[block]))
        copies[-1].start()
    table_copy = pltpu.make_async_copy(table_hbm, table_ref, sems.at[blocks])
    table_copy.start()

    for block in range(blocks):
        copies[block].wait()

        def fir_tile(nt, _, block=block):
            lane = pl.multiple_of(nt * LANES, LANES)
            taps = [taper_ref[t, :, pl.ds(lane, LANES)] for t in range(TAPS)]

            def load(frame):
                at = pl.multiple_of((block * FIR_BLOCK + frame) * NFFT + lane, LANES)
                return volts_ref[:, pl.ds(at, LANES)].astype(jnp.float32)

            held = [load(t) for t in range(HALO)]
            done = []
            for s in range(FIR_BLOCK):
                held.append(load(s + HALO))
                total = taps[0] * held[0]
                for t in range(1, TAPS):
                    total = total + taps[t] * held[t]
                held = held[1:]
                done.append(total)
            turned = jnp.swapaxes(jnp.stack(done, axis=0), 0, 1).astype(jnp.bfloat16)
            for i in range(OWN):
                frames_ref[pl.ds(i * SPECTRA + block * FIR_BLOCK, FIR_BLOCK), pl.ds(lane, LANES)] = turned[i]
            return 0

        lax.fori_loop(0, NT, fir_tile, 0)
    table_copy.wait()
    far, near = 1 - where_ref[0], where_ref[0]
    transform_block(table_ref[far, 0], frames_ref, turn_ref)
    place(turn_ref, first_ref, where_ref[1])
    copies = [pltpu.make_async_copy(first_ref, first_hbm, sems.at[blocks + 1])]
    copies[0].start()
    sent = first_ref.shape[1]
    for part, (plane, chunk) in enumerate(((far, 1), (near, 0), (near, 1))):
        transform_block(table_ref[plane, chunk], frames_ref, turn_ref)
        rows = pl.ds(part * sent, sent)
        place(turn_ref, rest_ref.at[:, rows, :], 0)
        copies.append(
            pltpu.make_async_copy(rest_ref.at[:, rows, :], rest_hbm.at[:, rows, :], sems.at[blocks + 2 + part])
        )
        copies[-1].start()
    for copy in copies:
        copy.wait()


def channelize(where, volts, table):
    taper = jnp.asarray(np.broadcast_to(taper_table()[:, None, :], (TAPS, OWN, NFFT)).copy())
    sent = table.shape[2] * OWN // PLANE
    first = jax.ShapeDtypeStruct((PLANE, sent, SPECTRA), jnp.bfloat16)
    rest = jax.ShapeDtypeStruct((PLANE, 3 * sent, SPECTRA), jnp.bfloat16)
    vmem, hbm = pl.BlockSpec(memory_space=pltpu.VMEM), pl.BlockSpec(memory_space=pl.ANY)
    return pl.pallas_call(
        channelize_kernel,
        out_shape=(first, rest),
        in_specs=[pl.BlockSpec(memory_space=pltpu.SMEM), hbm, vmem, hbm],
        out_specs=(hbm, hbm),
        scratch_shapes=[
            pltpu.VMEM(volts.shape, jnp.bfloat16),
            pltpu.VMEM(table.shape, jnp.bfloat16),
            pltpu.VMEM((SPECTRA * OWN, NFFT), jnp.bfloat16),
            pltpu.VMEM((table.shape[2] * OWN, SPECTRA), jnp.float32),
            pltpu.VMEM(first.shape, jnp.bfloat16),
            pltpu.VMEM(rest.shape, jnp.bfloat16),
            pltpu.SemaphoreType.DMA((SPECTRA // FIR_BLOCK + 5,)),
        ],
        compiler_params=pltpu.CompilerParams(vmem_limit_bytes=LARGE),
        cost_estimate=SHORT,
    )(where, volts, taper, table)


def one_hot(rows, columns):
    return jnp.where(rows == columns, 1.0, 0.0).astype(jnp.bfloat16)


def weight_kernel(swapped, where_ref, order_ref, map_ref, weights_ref, out_ref, pick_ref, place_ref):
    beams = weights_ref.shape[2]
    feeds = weights_ref.shape[3]
    z_hi, y_x, core, z_lo = (where_ref[k] for k in range(4))

    def iota(rows, columns, axis):
        return lax.broadcasted_iota(jnp.int32, (rows, columns), axis)

    def product(one, two, contract):
        return lax.dot_general(
            one, two, (((1,), (contract,)), ((), ())), preferred_element_type=jnp.float32
        ).astype(jnp.bfloat16)

    @pl.when(pl.program_id(0) == 0)
    def _():
        own = beams // 8
        block = iota(beams, beams, 0) // own
        position = ((block % 4) ^ z_lo) * 2 + ((block // 4) ^ core)
        position = position * own + iota(beams, beams, 0) % own
        chosen = one_hot(position, iota(beams, beams, 1))
        pick_ref[...] = product(chosen, one_hot(iota(beams, beams, 0), order_ref[...]), 1)
        at = iota(feeds, 2 * feeds, 1)
        entry = at // (2 * OWN) % PLANE
        is_imag = at // OWN % 2
        feed_of = one_hot(iota(feeds, feeds, 0), map_ref[...])
        y, x = entry // 4, entry % 4
        if swapped:
            far = at // feeds
            y, x = jnp.where(far == 1, entry % 4 ^ y_x // 4, y), jnp.where(far == 1, entry // 4 ^ y_x % 4, x)
        source = y * 8 + (at // feeds ^ z_hi) * 4 + x
        match = product(feed_of, one_hot(iota(feeds, 2 * feeds, 0), source * OWN + at % OWN), 0)
        place_ref[0:feeds] = jnp.where(is_imag == 0, match, jnp.zeros_like(match))
        place_ref[feeds:] = jnp.where(is_imag == 1, match, jnp.zeros_like(match))

    wide = jnp.concatenate([weights_ref[0, 0], weights_ref[0, 1]], axis=1)
    picked = product(pick_ref[...], wide, 0)
    out_ref[0] = product(picked, place_ref[...], 0)


def arrange_weights(where, weights, order, inputs_map, chunk):
    chans, _, beams, feeds = weights.shape
    chans //= 2
    return pl.pallas_call(
        functools.partial(weight_kernel, chunk == 0),
        grid_spec=pltpu.PrefetchScalarGridSpec(
            num_scalar_prefetch=1,
            grid=(chans,),
            in_specs=[
                pl.BlockSpec((1, beams), lambda c, w: (0, 0)),
                pl.BlockSpec((1, feeds), lambda c, w: (0, 0)),
                pl.BlockSpec((1, 2, beams, feeds), lambda c, w: (chunk * chans + c, 0, 0, 0)),
            ],
            out_specs=pl.BlockSpec((1, beams, 2 * feeds), lambda c, w: (c, 0, 0)),
            scratch_shapes=[
                pltpu.VMEM((beams, beams), jnp.bfloat16),
                pltpu.VMEM((2 * feeds, 2 * feeds), jnp.bfloat16),
            ],
        ),
        out_shape=jax.ShapeDtypeStruct((chans, beams, 2 * feeds), jnp.bfloat16),
        compiler_params=pltpu.CompilerParams(vmem_limit_bytes=SMALL),
        cost_estimate=SHORT,
    )(where, order.reshape(1, beams), inputs_map.reshape(1, feeds), weights)


def combine_kernel(turned, weights_ref, near_ref, far_ref, keep_ref, send_ref):
    beams = weights_ref.shape[1]
    spectra = near_ref.shape[3]
    half = beams // 2
    data = jnp.concatenate([near_ref[:, 0], far_ref[:, 0]], axis=0).astype(jnp.float32)
    real, imag = data[:, :OWN], data[:, OWN:]
    of_real = jnp.concatenate([real, -imag], axis=1).reshape(-1, spectra)
    of_imag = jnp.concatenate([imag, real], axis=1).reshape(-1, spectra)
    both = jnp.concatenate([of_real, of_imag], axis=1).astype(jnp.bfloat16)
    product = jnp.dot(weights_ref[0], both, preferred_element_type=jnp.float32)
    for part in range(2):
        mine = product[:, part * spectra : (part + 1) * spectra]
        quarter = half // 4
        for block in range(4):
            at = (block % 2, block // 2) if turned else (block // 2, block % 2)
            rows = slice(block * quarter, (block + 1) * quarter)
            keep_ref[at[0], at[1], 0, part] = mine[:half][rows]
            send_ref[at[0], at[1], 0, part] = mine[half:][rows].astype(jnp.bfloat16)


def combine(arranged, near, near_from, far, chunk):
    beams, wide = arranged.shape[1:]
    sources, chans, rows, spectra = far.shape
    shape = (2, 2, chans, 2, beams // 8, spectra)
    block = pl.BlockSpec((2, 2, 1, 2, beams // 8, spectra), lambda c: (0, 0, c, 0, 0, 0))
    return pl.pallas_call(
        functools.partial(combine_kernel, chunk == 1),
        grid=(chans,),
        out_shape=(jax.ShapeDtypeStruct(shape, jnp.float32), jax.ShapeDtypeStruct(shape, jnp.bfloat16)),
        in_specs=[
            pl.BlockSpec((1, beams, wide), lambda c: (c, 0, 0)),
            pl.BlockSpec((sources, 1, rows, spectra), lambda c: (0, near_from + c, 0, 0)),
            pl.BlockSpec((sources, 1, rows, spectra), lambda c: (0, c, 0, 0)),
        ],
        out_specs=(block, block),
        compiler_params=pltpu.CompilerParams(vmem_limit_bytes=SMALL),
        cost_estimate=SHORT,
    )(arranged, near, far)


def fine_tables():
    steps = np.arange(UPCH)
    angles = 2.0 * math.pi * (np.outer(steps, steps) % UPCH) / UPCH
    eye = np.eye(SPECTRA // UPCH)
    real = np.kron(eye, np.cos(angles) / math.sqrt(UPCH))
    imag = np.kron(eye, -np.sin(angles) / math.sqrt(UPCH))
    turn = np.block([[real, imag], [-imag, real]]).astype(np.float32)
    mean = np.tile(np.eye(UPCH) * UPCH / SPECTRA, (1, SPECTRA // UPCH)).astype(np.float32)
    high = turn.astype(jnp.bfloat16)
    low = (turn - high.astype(np.float32)).astype(jnp.bfloat16)
    return np.stack([high, low]), mean


def three_products(value, high, low):
    top = value.astype(jnp.bfloat16)
    rest = (value - top.astype(jnp.float32)).astype(jnp.bfloat16)
    wide = jnp.float32
    total = jnp.dot(top, low, preferred_element_type=wide) + jnp.dot(rest, high, preferred_element_type=wide)
    return total + jnp.dot(top, high, preferred_element_type=wide)


def detect_kernel(*refs):
    halves, (turn_ref, mean_ref, out_ref) = refs[:-3], refs[-3:]
    wide = jnp.float32
    for at in range(0, len(halves), 4):
        keep_ref, come_ref, one_ref, two_ref = halves[at : at + 4]
        total = keep_ref[0, 0] + come_ref[0, 0].astype(wide) + one_ref[0].astype(wide) + two_ref[...].astype(wide)
        chans, _, beams, spectra = total.shape
        both = jnp.concatenate(
            [total[:, 0].reshape(chans * beams, spectra), total[:, 1].reshape(chans * beams, spectra)], axis=1
        )
        sub = three_products(both, turn_ref[0], turn_ref[1])
        power = sub[:, :spectra] * sub[:, :spectra] + sub[:, spectra:] * sub[:, spectra:]
        mean = lax.dot_general(
            mean_ref[...], power, (((1,), (1,)), ((), ())), preferred_element_type=wide, precision=lax.Precision.HIGHEST
        )
        for chan in range(chans):
            out_ref[at // 4 * chans + chan] = mean[:, chan * beams : (chan + 1) * beams]


def detect(halves):
    chans, _, beams, spectra = halves[0][0].shape[2:]
    turn, mean = fine_tables()
    block = (chans, 2, beams, spectra)
    corner = pl.BlockSpec((1, 1) + block, lambda k: (0,) * 6)
    one = pl.BlockSpec((1,) + block, lambda k: (0,) * 5)
    two = pl.BlockSpec(block, lambda k: (0,) * 4)
    whole = pl.BlockSpec(memory_space=pltpu.VMEM)
    return pl.pallas_call(
        detect_kernel,
        grid=(1,),
        out_shape=jax.ShapeDtypeStruct((len(halves) * chans, UPCH, beams), jnp.float32),
        in_specs=[corner, corner, one, two] * len(halves) + [whole] * 2,
        out_specs=whole,
        compiler_params=pltpu.CompilerParams(vmem_limit_bytes=SMALL),
        cost_estimate=SHORT,
    )(*[part for half in halves for part in half], jnp.asarray(turn), jnp.asarray(mean))


def swap(value, axis, distance, size):
    return lax.ppermute(value, axis, [(k, k ^ distance) for k in range(size)])


def after(value, earlier):
    return lax.optimization_barrier((value, earlier))[0]


def narrow(value):
    return value.astype(jnp.bfloat16)


def widen(value):
    return value.astype(jnp.float32)


def channel_table(chans):
    rows = transform_table().reshape(4, 2, 4, 2, chans, NFFT)
    return jnp.asarray(np.transpose(rows, (1, 3, 0, 2, 4, 5)).reshape(2, 2, 16 * chans, NFFT))


def on_device(voltages, weights, input_map, beam_order):
    chans = weights.shape[0]
    half = chans // 2
    table = channel_table(chans)
    z_hi = lax.axis_index("zh")
    y, x = lax.axis_index("y"), lax.axis_index("x")
    core, z = lax.axis_index("core"), lax.axis_index("zl")
    where = jnp.stack([z_hi, 4 * y + x, core, z]).astype(jnp.int32)

    def turn_by_swaps(value):
        value = value.reshape(4, 4, -1, SPECTRA)
        rows = [value[0]] + [swap(value[k], "y", k, 4) for k in (1, 2, 3)]
        columns = [jnp.stack([row[k] for row in rows]) for k in range(4)]
        columns = [columns[0]] + [swap(columns[k], "x", k, 4) for k in (1, 2, 3)]
        return jnp.stack(columns).reshape(PLANE, -1, 2 * OWN, SPECTRA)

    def turn(value):
        value = lax.all_to_all(value.reshape(PLANE, -1, SPECTRA), ("y", "x"), split_axis=0, concat_axis=0, tiled=True)
        return value.reshape(PLANE, -1, 2 * OWN, SPECTRA)

    first, rest = channelize(where, voltages, table)
    far0 = swap(first, "zh", 1, 2)
    planed = turn(rest)
    far1 = swap(planed[:, :half], "zh", 1, 2)
    arranged0 = arrange_weights(where, after(weights, rest), beam_order, input_map, 0)
    arranged1 = arrange_weights(where, after(after(weights, planed), arranged0), beam_order, input_map, 1)
    data0 = after(turn_by_swaps(after(far0, arranged1)), far1)

    keep0, send0 = combine(arranged0, planed, half, data0, 0)
    come0 = swap(send0, "core", 1, 2)
    to0 = narrow(keep0[1] + widen(come0[1]))
    keep1, send1 = combine(arranged1, planed, 2 * half, far1, 1)
    come1 = swap(send1, "core", 1, 2)
    one0 = swap(to0, "zl", 2, 4)
    one1 = swap(narrow(keep1[1] + widen(come1[1])), "zl", 1, 4)
    two0 = swap(narrow(keep0[0, 1] + widen(come0[0, 1]) + widen(one0[1])), "zl", 1, 4)
    two1 = swap(narrow(keep1[0, 1] + widen(come1[0, 1]) + widen(one1[1])), "zl", 2, 4)
    return detect([(keep0, come0, one0, two0), (keep1, come1, one1, two1)])


def solution(mesh):
    fine = Mesh(mesh.devices.reshape(4, 2, 4, 2, 4), ("zl", "core", "y", "zh", "x"))
    grp, dev = ("zl", "core"), ("y", "zh", "x")
    placed = (P(grp + dev, None), P(dev, None, None, grp), P(grp), P())
    return jax.shard_map(on_device, mesh=fine, in_specs=placed, out_specs=P(dev, None, grp), check_vma=False)
```

```python
import functools
import math

import jax
import jax.numpy as jnp
import numpy as np
from jax import lax
from jax.experimental import pallas as pl
from jax.experimental.pallas import tpu as pltpu
from jax.sharding import Mesh
from jax.sharding import PartitionSpec as P

CHAN = 1024
NFFT = 2048
TAPS = 4
UPCH = 16
WIN = 512
SPECTRA = 128
BAND_LO = 256
LANES = 128
OWN = 8
NT = NFFT // LANES
LARGE, SMALL = 60 << 20, 16 << 20
SHORT = pl.CostEstimate(flops=1, bytes_accessed=1, transcendentals=0)


def taper_table():
    index = np.arange(TAPS * NFFT, dtype=np.float64)
    centred = (index - TAPS * NFFT / 2.0 + 0.5) / NFFT
    window = 0.5 - 0.5 * np.cos(2.0 * math.pi * (index + 0.5) / (TAPS * NFFT))
    return (np.sinc(centred) * window).astype(np.float32).reshape(TAPS, NFFT)


def transform_table():
    chan_ids = BAND_LO + np.arange(WIN)
    angles = 2.0 * math.pi * ((chan_ids[:, None] * np.arange(NFFT)[None, :]) % NFFT) / NFFT
    stacked = np.stack([np.cos(angles), -np.sin(angles)], axis=1) / math.sqrt(CHAN)
    return stacked.reshape(2 * WIN, NFFT).astype(jnp.bfloat16)


FIR_BLOCK = 32
HALO = TAPS - 1


def transform_block(table, frames_ref, turn_ref):
    rows = table.shape[0]
    for pair in range(OWN // 2):
        part = lax.dot_general(
            table,
            frames_ref[pl.ds(pair * 2 * SPECTRA, 2 * SPECTRA), :],
            (((1,), (1,)), ((), ())),
            preferred_element_type=jnp.float32,
        )
        for half in range(2):
            turn_ref[pl.ds(pair * 2 + half, rows, stride=OWN), :] = part[:, half * SPECTRA : (half + 1) * SPECTRA]


PLANE = 16


def place(turn_ref, out_ref, mine):
    rows = turn_ref.shape[0] // PLANE
    for owner in range(PLANE):
        out_ref[mine ^ owner] = turn_ref[owner * rows : (owner + 1) * rows, :].astype(jnp.bfloat16)


def channelize_kernel(
    where_ref, volts_hbm, taper_ref, table_hbm, first_hbm, rest_hbm,
    volts_ref, table_ref, frames_ref, turn_ref, first_ref, rest_ref, sems,
):
    blocks = SPECTRA // FIR_BLOCK
    copies = []
    for block in range(blocks):
        first = block * FIR_BLOCK + (HALO if block else 0)
        last = (block + 1) * FIR_BLOCK + HALO
        span = pl.ds(first * NFFT, (last - first) * NFFT)
        copies.append(pltpu.make_async_copy(volts_hbm.at[:, span], volts_ref.at[:, span], sems.at[block]))
        copies[-1].start()
    table_copy = pltpu.make_async_copy(table_hbm, table_ref, sems.at[blocks])
    table_copy.start()

    for block in range(blocks):
        copies[block].wait()

        def fir_tile(nt, _, block=block):
            lane = pl.multiple_of(nt * LANES, LANES)
            taps = [taper_ref[t, :, pl.ds(lane, LANES)] for t in range(TAPS)]

            def load(frame):
                at = pl.multiple_of((block * FIR_BLOCK + frame) * NFFT + lane, LANES)
                return volts_ref[:, pl.ds(at, LANES)].astype(jnp.float32)

            held = [load(t) for t in range(HALO)]
            done = []
            for s in range(FIR_BLOCK):
                held.append(load(s + HALO))
                total = taps[0] * held[0]
                for t in range(1, TAPS):
                    total = total + taps[t] * held[t]
                held = held[1:]
                done.append(total)
            turned = jnp.swapaxes(jnp.stack(done, axis=0), 0, 1).astype(jnp.bfloat16)
            for i in range(OWN):
                frames_ref[pl.ds(i * SPECTRA + block * FIR_BLOCK, FIR_BLOCK), pl.ds(lane, LANES)] = turned[i]
            return 0

        lax.fori_loop(0, NT, fir_tile, 0)
    table_copy.wait()
    far, near = 1 - where_ref[0], where_ref[0]
    transform_block(table_ref[far, 0], frames_ref, turn_ref)
    place(turn_ref, first_ref, where_ref[1])
    copies = [pltpu.make_async_copy(first_ref, first_hbm, sems.at[blocks + 1])]
    copies[0].start()
    sent = first_ref.shape[1]
    for part, (plane, chunk) in enumerate(((far, 1), (near, 0), (near, 1))):
        transform_block(table_ref[plane, chunk], frames_ref, turn_ref)
        rows = pl.ds(part * sent, sent)
        place(turn_ref, rest_ref.at[:, rows, :], 0)
        copies.append(
            pltpu.make_async_copy(rest_ref.at[:, rows, :], rest_hbm.at[:, rows, :], sems.at[blocks + 2 + part])
        )
        copies[-1].start()
    for copy in copies:
        copy.wait()


def channelize(where, volts, table):
    taper = jnp.asarray(np.broadcast_to(taper_table()[:, None, :], (TAPS, OWN, NFFT)).copy())
    sent = table.shape[2] * OWN // PLANE
    first = jax.ShapeDtypeStruct((PLANE, sent, SPECTRA), jnp.bfloat16)
    rest = jax.ShapeDtypeStruct((PLANE, 3 * sent, SPECTRA), jnp.bfloat16)
    vmem, hbm = pl.BlockSpec(memory_space=pltpu.VMEM), pl.BlockSpec(memory_space=pl.ANY)
    return pl.pallas_call(
        channelize_kernel,
        out_shape=(first, rest),
        in_specs=[pl.BlockSpec(memory_space=pltpu.SMEM), hbm, vmem, hbm],
        out_specs=(hbm, hbm),
        scratch_shapes=[
            pltpu.VMEM(volts.shape, jnp.bfloat16),
            pltpu.VMEM(table.shape, jnp.bfloat16),
            pltpu.VMEM((SPECTRA * OWN, NFFT), jnp.bfloat16),
            pltpu.VMEM((table.shape[2] * OWN, SPECTRA), jnp.float32),
            pltpu.VMEM(first.shape, jnp.bfloat16),
            pltpu.VMEM(rest.shape, jnp.bfloat16),
            pltpu.SemaphoreType.DMA((SPECTRA // FIR_BLOCK + 5,)),
        ],
        compiler_params=pltpu.CompilerParams(vmem_limit_bytes=LARGE),
        cost_estimate=SHORT,
    )(where, volts, taper, table)


def one_hot(rows, columns):
    return jnp.where(rows == columns, 1.0, 0.0).astype(jnp.bfloat16)


def weight_kernel(swapped, where_ref, order_ref, map_ref, weights_ref, out_ref, pick_ref, place_ref):
    beams = weights_ref.shape[2]
    feeds = weights_ref.shape[3]
    z_hi, y_x, core, z_lo = (where_ref[k] for k in range(4))

    def iota(rows, columns, axis):
        return lax.broadcasted_iota(jnp.int32, (rows, columns), axis)

    def product(one, two, contract):
        return lax.dot_general(
            one, two, (((1,), (contract,)), ((), ())), preferred_element_type=jnp.float32
        ).astype(jnp.bfloat16)

    @pl.when(pl.program_id(0) == 0)
    def _():
        own = beams // 8
        block = iota(beams, beams, 0) // own
        position = ((block % 4) ^ z_lo) * 2 + ((block // 4) ^ core)
        position = position * own + iota(beams, beams, 0) % own
        chosen = one_hot(position, iota(beams, beams, 1))
        pick_ref[...] = product(chosen, one_hot(iota(beams, beams, 0), order_ref[...]), 1)
        at = iota(feeds, 2 * feeds, 1)
        entry = at // (2 * OWN) % PLANE
        is_imag = at // OWN % 2
        feed_of = one_hot(iota(feeds, feeds, 0), map_ref[...])
        y, x = entry // 4, entry % 4
        if swapped:
            far = at // feeds
            y, x = jnp.where(far == 1, entry % 4 ^ y_x // 4, y), jnp.where(far == 1, entry // 4 ^ y_x % 4, x)
        source = y * 8 + (at // feeds ^ z_hi) * 4 + x
        match = product(feed_of, one_hot(iota(feeds, 2 * feeds, 0), source * OWN + at % OWN), 0)
        place_ref[0:feeds] = jnp.where(is_imag == 0, match, jnp.zeros_like(match))
        place_ref[feeds:] = jnp.where(is_imag == 1, match, jnp.zeros_like(match))

    for chan in range(weights_ref.shape[0]):
        wide = jnp.concatenate([weights_ref[chan, 0], weights_ref[chan, 1]], axis=1)
        picked = product(pick_ref[...], wide, 0)
        out_ref[chan] = product(picked, place_ref[...], 0)


PER_STEP = 2


def arrange_weights(where, weights, order, inputs_map, chunk):
    chans, _, beams, feeds = weights.shape
    chans //= 2
    return pl.pallas_call(
        functools.partial(weight_kernel, chunk == 0),
        grid_spec=pltpu.PrefetchScalarGridSpec(
            num_scalar_prefetch=1,
            grid=(chans // PER_STEP,),
            in_specs=[
                pl.BlockSpec((1, beams), lambda c, w: (0, 0)),
                pl.BlockSpec((1, feeds), lambda c, w: (0, 0)),
                pl.BlockSpec((PER_STEP, 2, beams, feeds), lambda c, w: (chunk * chans // PER_STEP + c, 0, 0, 0)),
            ],
            out_specs=pl.BlockSpec((PER_STEP, beams, 2 * feeds), lambda c, w: (c, 0, 0)),
            scratch_shapes=[
                pltpu.VMEM((beams, beams), jnp.bfloat16),
                pltpu.VMEM((2 * feeds, 2 * feeds), jnp.bfloat16),
            ],
        ),
        out_shape=jax.ShapeDtypeStruct((chans, beams, 2 * feeds), jnp.bfloat16),
        compiler_params=pltpu.CompilerParams(vmem_limit_bytes=LARGE),
        cost_estimate=SHORT,
    )(where, order.reshape(1, beams), inputs_map.reshape(1, feeds), weights)


def combine_kernel(turned, weights_ref, near_ref, far_ref, keep_ref, send_ref):
    beams = weights_ref.shape[1]
    spectra = near_ref.shape[3]
    half = beams // 2
    data = jnp.concatenate([near_ref[:, 0], far_ref[:, 0]], axis=0).astype(jnp.float32)
    real, imag = data[:, :OWN], data[:, OWN:]
    of_real = jnp.concatenate([real, -imag], axis=1).reshape(-1, spectra)
    of_imag = jnp.concatenate([imag, real], axis=1).reshape(-1, spectra)
    both = jnp.concatenate([of_real, of_imag], axis=1).astype(jnp.bfloat16)
    product = jnp.dot(weights_ref[0], both, preferred_element_type=jnp.float32)
    for part in range(2):
        mine = product[:, part * spectra : (part + 1) * spectra]
        quarter = half // 4
        for block in range(4):
            at = (block % 2, block // 2) if turned else (block // 2, block % 2)
            rows = slice(block * quarter, (block + 1) * quarter)
            keep_ref[at[0], at[1], 0, part] = mine[:half][rows]
            send_ref[at[0], at[1], 0, part] = mine[half:][rows].astype(jnp.bfloat16)


def combine(arranged, near, near_from, far, chunk):
    beams, wide = arranged.shape[1:]
    sources, chans, rows, spectra = far.shape
    shape = (2, 2, chans, 2, beams // 8, spectra)
    block = pl.BlockSpec((2, 2, 1, 2, beams // 8, spectra), lambda c: (0, 0, c, 0, 0, 0))
    return pl.pallas_call(
        functools.partial(combine_kernel, chunk == 1),
        grid=(chans,),
        out_shape=(jax.ShapeDtypeStruct(shape, jnp.float32), jax.ShapeDtypeStruct(shape, jnp.bfloat16)),
        in_specs=[
            pl.BlockSpec((1, beams, wide), lambda c: (c, 0, 0)),
            pl.BlockSpec((sources, 1, rows, spectra), lambda c: (0, near_from + c, 0, 0)),
            pl.BlockSpec((sources, 1, rows, spectra), lambda c: (0, c, 0, 0)),
        ],
        out_specs=(block, block),
        compiler_params=pltpu.CompilerParams(vmem_limit_bytes=SMALL),
        cost_estimate=SHORT,
    )(arranged, near, far)


def fine_tables():
    steps = np.arange(UPCH)
    angles = 2.0 * math.pi * (np.outer(steps, steps) % UPCH) / UPCH
    eye = np.eye(SPECTRA // UPCH)
    real = np.kron(eye, np.cos(angles) / math.sqrt(UPCH))
    imag = np.kron(eye, -np.sin(angles) / math.sqrt(UPCH))
    turn = np.block([[real, imag], [-imag, real]]).astype(np.float32)
    mean = np.tile(np.eye(UPCH) * UPCH / SPECTRA, (1, SPECTRA // UPCH)).astype(np.float32)
    high = turn.astype(jnp.bfloat16)
    low = (turn - high.astype(np.float32)).astype(jnp.bfloat16)
    return np.stack([high, low]), mean


def three_products(value, high, low):
    top = value.astype(jnp.bfloat16)
    rest = (value - top.astype(jnp.float32)).astype(jnp.bfloat16)
    wide = jnp.float32
    total = jnp.dot(top, low, preferred_element_type=wide) + jnp.dot(rest, high, preferred_element_type=wide)
    return total + jnp.dot(top, high, preferred_element_type=wide)


def detect_kernel(*refs):
    halves, (turn_ref, mean_ref, out_ref) = refs[:-3], refs[-3:]
    wide = jnp.float32
    for at in range(0, len(halves), 4):
        keep_ref, come_ref, one_ref, two_ref = halves[at : at + 4]
        total = keep_ref[0, 0] + come_ref[0, 0].astype(wide) + one_ref[0].astype(wide) + two_ref[...].astype(wide)
        chans, _, beams, spectra = total.shape
        both = jnp.concatenate(
            [total[:, 0].reshape(chans * beams, spectra), total[:, 1].reshape(chans * beams, spectra)], axis=1
        )
        sub = three_products(both, turn_ref[0], turn_ref[1])
        power = sub[:, :spectra] * sub[:, :spectra] + sub[:, spectra:] * sub[:, spectra:]
        mean = lax.dot_general(
            mean_ref[...], power, (((1,), (1,)), ((), ())), preferred_element_type=wide, precision=lax.Precision.HIGHEST
        )
        for chan in range(chans):
            out_ref[at // 4 * chans + chan] = mean[:, chan * beams : (chan + 1) * beams]


def detect(halves):
    chans, _, beams, spectra = halves[0][0].shape[2:]
    turn, mean = fine_tables()
    block = (chans, 2, beams, spectra)
    corner = pl.BlockSpec((1, 1) + block, lambda k: (0,) * 6)
    one = pl.BlockSpec((1,) + block, lambda k: (0,) * 5)
    two = pl.BlockSpec(block, lambda k: (0,) * 4)
    whole = pl.BlockSpec(memory_space=pltpu.VMEM)
    return pl.pallas_call(
        detect_kernel,
        grid=(1,),
        out_shape=jax.ShapeDtypeStruct((len(halves) * chans, UPCH, beams), jnp.float32),
        in_specs=[corner, corner, one, two] * len(halves) + [whole] * 2,
        out_specs=whole,
        compiler_params=pltpu.CompilerParams(vmem_limit_bytes=SMALL),
        cost_estimate=SHORT,
    )(*[part for half in halves for part in half], jnp.asarray(turn), jnp.asarray(mean))


def swap(value, axis, distance, size):
    return lax.ppermute(value, axis, [(k, k ^ distance) for k in range(size)])


def after(value, earlier):
    return lax.optimization_barrier((value, earlier))[0]


def narrow(value):
    return value.astype(jnp.bfloat16)


def widen(value):
    return value.astype(jnp.float32)


def channel_table(chans):
    rows = transform_table().reshape(4, 2, 4, 2, chans, NFFT)
    return jnp.asarray(np.transpose(rows, (1, 3, 0, 2, 4, 5)).reshape(2, 2, 16 * chans, NFFT))


def on_device(voltages, weights, input_map, beam_order):
    chans = weights.shape[0]
    half = chans // 2
    table = channel_table(chans)
    z_hi = lax.axis_index("zh")
    y, x = lax.axis_index("y"), lax.axis_index("x")
    core, z = lax.axis_index("core"), lax.axis_index("zl")
    where = jnp.stack([z_hi, 4 * y + x, core, z]).astype(jnp.int32)

    def turn_by_swaps(value):
        value = value.reshape(4, 4, -1, SPECTRA)
        rows = [value[0]] + [swap(value[k], "y", k, 4) for k in (1, 2, 3)]
        columns = [jnp.stack([row[k] for row in rows]) for k in range(4)]
        columns = [columns[0]] + [swap(columns[k], "x", k, 4) for k in (1, 2, 3)]
        return jnp.stack(columns).reshape(PLANE, -1, 2 * OWN, SPECTRA)

    def turn(value):
        value = lax.all_to_all(value.reshape(PLANE, -1, SPECTRA), ("y", "x"), split_axis=0, concat_axis=0, tiled=True)
        return value.reshape(PLANE, -1, 2 * OWN, SPECTRA)

    first, rest = channelize(where, voltages, table)
    far0 = swap(first, "zh", 1, 2)
    planed = turn(rest)
    far1 = swap(planed[:, :half], "zh", 1, 2)
    arranged0 = arrange_weights(where, after(weights, rest), beam_order, input_map, 0)
    arranged1 = arrange_weights(where, after(weights, arranged0), beam_order, input_map, 1)
    data0 = after(turn_by_swaps(after(after(far0, arranged1), planed)), far1)

    keep0, send0 = combine(arranged0, planed, half, data0, 0)
    come0 = swap(send0, "core", 1, 2)
    to0 = narrow(keep0[1] + widen(come0[1]))
    keep1, send1 = combine(arranged1, planed, 2 * half, far1, 1)
    come1 = swap(send1, "core", 1, 2)
    one0 = swap(to0, "zl", 2, 4)
    one1 = swap(narrow(keep1[1] + widen(come1[1])), "zl", 1, 4)
    two0 = swap(narrow(keep0[0, 1] + widen(come0[0, 1]) + widen(one0[1])), "zl", 1, 4)
    two1 = swap(narrow(keep1[0, 1] + widen(come1[0, 1]) + widen(one1[1])), "zl", 2, 4)
    return detect([(keep0, come0, one0, two0), (keep1, come1, one1, two1)])


def solution(mesh):
    fine = Mesh(mesh.devices.reshape(4, 2, 4, 2, 4), ("zl", "core", "y", "zh", "x"))
    grp, dev = ("zl", "core"), ("y", "zh", "x")
    placed = (P(grp + dev, None), P(dev, None, None, grp), P(grp), P())
    return jax.shard_map(on_device, mesh=fine, in_specs=placed, out_specs=P(dev, None, grp), check_vma=False)
```

```python
import functools
import math

import jax
import jax.numpy as jnp
import numpy as np
from jax import lax
from jax.experimental import pallas as pl
from jax.experimental.pallas import tpu as pltpu
from jax.sharding import Mesh
from jax.sharding import PartitionSpec as P

CHAN = 1024
NFFT = 2048
TAPS = 4
UPCH = 16
WIN = 512
SPECTRA = 128
BAND_LO = 256
LANES = 128
OWN = 8
NT = NFFT // LANES
LARGE, SMALL = 60 << 20, 16 << 20
SHORT = pl.CostEstimate(flops=1, bytes_accessed=1, transcendentals=0)


def taper_table():
    index = np.arange(TAPS * NFFT, dtype=np.float64)
    centred = (index - TAPS * NFFT / 2.0 + 0.5) / NFFT
    window = 0.5 - 0.5 * np.cos(2.0 * math.pi * (index + 0.5) / (TAPS * NFFT))
    return (np.sinc(centred) * window).astype(np.float32).reshape(TAPS, NFFT)


def transform_table():
    chan_ids = BAND_LO + np.arange(WIN)
    angles = 2.0 * math.pi * ((chan_ids[:, None] * np.arange(NFFT)[None, :]) % NFFT) / NFFT
    stacked = np.stack([np.cos(angles), -np.sin(angles)], axis=1) / math.sqrt(CHAN)
    return stacked.reshape(2 * WIN, NFFT).astype(jnp.bfloat16)


FIR_BLOCK = 32
HALO = TAPS - 1


def transform_block(table, frames_ref, turn_ref):
    rows = table.shape[0]
    for pair in range(OWN // 2):
        part = lax.dot_general(
            table,
            frames_ref[pl.ds(pair * 2 * SPECTRA, 2 * SPECTRA), :],
            (((1,), (1,)), ((), ())),
            preferred_element_type=jnp.float32,
        )
        for half in range(2):
            turn_ref[pl.ds(pair * 2 + half, rows, stride=OWN), :] = part[:, half * SPECTRA : (half + 1) * SPECTRA]


PLANE = 16


def place(turn_ref, out_ref, mine):
    rows = turn_ref.shape[0] // PLANE
    for owner in range(PLANE):
        out_ref[mine ^ owner] = turn_ref[owner * rows : (owner + 1) * rows, :].astype(jnp.bfloat16)


def channelize_kernel(
    volts_hbm, taper_ref, table_hbm, first_hbm, rest_hbm,
    volts_ref, table_ref, frames_ref, turn_ref, first_ref, rest_ref, sems,
):
    blocks = SPECTRA // FIR_BLOCK
    copies = []
    for block in range(blocks):
        first = block * FIR_BLOCK + (HALO if block else 0)
        last = (block + 1) * FIR_BLOCK + HALO
        span = pl.ds(first * NFFT, (last - first) * NFFT)
        copies.append(pltpu.make_async_copy(volts_hbm.at[:, span], volts_ref.at[:, span], sems.at[block]))
        copies[-1].start()
    table_copy = pltpu.make_async_copy(table_hbm, table_ref, sems.at[blocks])

    for block in range(blocks):
        copies[block].wait()
        if block == 0:
            table_copy.start()

        def fir_tile(nt, _, block=block):
            lane = pl.multiple_of(nt * LANES, LANES)
            taps = [taper_ref[t, :, pl.ds(lane, LANES)] for t in range(TAPS)]

            def load(frame):
                at = pl.multiple_of((block * FIR_BLOCK + frame) * NFFT + lane, LANES)
                return volts_ref[:, pl.ds(at, LANES)].astype(jnp.float32)

            held = [load(t) for t in range(HALO)]
            done = []
            for s in range(FIR_BLOCK):
                held.append(load(s + HALO))
                total = taps[0] * held[0]
                for t in range(1, TAPS):
                    total = total + taps[t] * held[t]
                held = held[1:]
                done.append(total)
            turned = jnp.swapaxes(jnp.stack(done, axis=0), 0, 1).astype(jnp.bfloat16)
            for i in range(OWN):
                frames_ref[pl.ds(i * SPECTRA + block * FIR_BLOCK, FIR_BLOCK), pl.ds(lane, LANES)] = turned[i]
            return 0

        lax.fori_loop(0, NT, fir_tile, 0)
    table_copy.wait()
    near = lax.axis_index("zh")
    far, plane_id = 1 - near, 4 * lax.axis_index("y") + lax.axis_index("x")
    transform_block(table_ref[far, 0], frames_ref, turn_ref)
    place(turn_ref, first_ref, plane_id)
    copies = [pltpu.make_async_copy(first_ref, first_hbm, sems.at[blocks + 1])]
    copies[0].start()
    sent = first_ref.shape[1]
    for part, (plane, chunk) in enumerate(((far, 1), (near, 0), (near, 1))):
        transform_block(table_ref[plane, chunk], frames_ref, turn_ref)
        rows = pl.ds(part * sent, sent)
        place(turn_ref, rest_ref.at[:, rows, :], 0)
        copies.append(
            pltpu.make_async_copy(rest_ref.at[:, rows, :], rest_hbm.at[:, rows, :], sems.at[blocks + 2 + part])
        )
        copies[-1].start()
    for copy in copies:
        copy.wait()


def channelize(volts, table):
    taper = jnp.asarray(np.broadcast_to(taper_table()[:, None, :], (TAPS, OWN, NFFT)).copy())
    sent = table.shape[2] * OWN // PLANE
    first = jax.ShapeDtypeStruct((PLANE, sent, SPECTRA), jnp.bfloat16)
    rest = jax.ShapeDtypeStruct((PLANE, 3 * sent, SPECTRA), jnp.bfloat16)
    vmem, hbm = pl.BlockSpec(memory_space=pltpu.VMEM), pl.BlockSpec(memory_space=pl.ANY)
    return pl.pallas_call(
        channelize_kernel,
        out_shape=(first, rest),
        in_specs=[hbm, vmem, hbm],
        out_specs=(hbm, hbm),
        scratch_shapes=[
            pltpu.VMEM(volts.shape, jnp.bfloat16),
            pltpu.VMEM(table.shape, jnp.bfloat16),
            pltpu.VMEM((SPECTRA * OWN, NFFT), jnp.bfloat16),
            pltpu.VMEM((table.shape[2] * OWN, SPECTRA), jnp.float32),
            pltpu.VMEM(first.shape, jnp.bfloat16),
            pltpu.VMEM(rest.shape, jnp.bfloat16),
            pltpu.SemaphoreType.DMA((SPECTRA // FIR_BLOCK + 5,)),
        ],
        compiler_params=pltpu.CompilerParams(vmem_limit_bytes=LARGE),
        cost_estimate=SHORT,
    )(volts, taper, table)


def one_hot(rows, columns):
    return jnp.where(rows == columns, 1.0, 0.0).astype(jnp.bfloat16)


def weight_kernel(swapped, where_ref, order_ref, map_ref, weights_ref, out_ref, pick_ref, place_ref):
    beams = weights_ref.shape[2]
    feeds = weights_ref.shape[3]
    z_hi, y_x, core, z_lo = (where_ref[k] for k in range(4))

    def iota(rows, columns, axis):
        return lax.broadcasted_iota(jnp.int32, (rows, columns), axis)

    def product(one, two, contract):
        return lax.dot_general(
            one, two, (((1,), (contract,)), ((), ())), preferred_element_type=jnp.float32
        ).astype(jnp.bfloat16)

    @pl.when(pl.program_id(0) == 0)
    def _():
        own = beams // 8
        block = iota(beams, beams, 0) // own
        position = ((block % 4) ^ z_lo) * 2 + ((block // 4) ^ core)
        position = position * own + iota(beams, beams, 0) % own
        chosen = one_hot(position, iota(beams, beams, 1))
        pick_ref[...] = product(chosen, one_hot(iota(beams, beams, 0), order_ref[...]), 1)
        at = iota(feeds, 2 * feeds, 1)
        entry = at // (2 * OWN) % PLANE
        is_imag = at // OWN % 2
        feed_of = one_hot(iota(feeds, feeds, 0), map_ref[...])
        y, x = entry // 4, entry % 4
        if swapped:
            far = at // feeds
            y, x = jnp.where(far == 1, entry % 4 ^ y_x // 4, y), jnp.where(far == 1, entry // 4 ^ y_x % 4, x)
        source = y * 8 + (at // feeds ^ z_hi) * 4 + x
        match = product(feed_of, one_hot(iota(feeds, 2 * feeds, 0), source * OWN + at % OWN), 0)
        place_ref[0:feeds] = jnp.where(is_imag == 0, match, jnp.zeros_like(match))
        place_ref[feeds:] = jnp.where(is_imag == 1, match, jnp.zeros_like(match))

    for chan in range(weights_ref.shape[0]):
        wide = jnp.concatenate([weights_ref[chan, 0], weights_ref[chan, 1]], axis=1)
        picked = product(pick_ref[...], wide, 0)
        out_ref[chan] = product(picked, place_ref[...], 0)


PER_STEP = 2


def arrange_weights(where, weights, order, inputs_map, chunk):
    chans, _, beams, feeds = weights.shape
    chans //= 2
    return pl.pallas_call(
        functools.partial(weight_kernel, chunk == 0),
        grid_spec=pltpu.PrefetchScalarGridSpec(
            num_scalar_prefetch=1,
            grid=(chans // PER_STEP,),
            in_specs=[
                pl.BlockSpec((1, beams), lambda c, w: (0, 0)),
                pl.BlockSpec((1, feeds), lambda c, w: (0, 0)),
                pl.BlockSpec((PER_STEP, 2, beams, feeds), lambda c, w: (chunk * chans // PER_STEP + c, 0, 0, 0)),
            ],
            out_specs=pl.BlockSpec((PER_STEP, beams, 2 * feeds), lambda c, w: (c, 0, 0)),
            scratch_shapes=[
                pltpu.VMEM((beams, beams), jnp.bfloat16),
                pltpu.VMEM((2 * feeds, 2 * feeds), jnp.bfloat16),
            ],
        ),
        out_shape=jax.ShapeDtypeStruct((chans, beams, 2 * feeds), jnp.bfloat16),
        compiler_params=pltpu.CompilerParams(vmem_limit_bytes=LARGE),
        cost_estimate=SHORT,
    )(where, order.reshape(1, beams), inputs_map.reshape(1, feeds), weights)


def combine_kernel(turned, weights_ref, near_ref, far_ref, keep_ref, send_ref):
    beams = weights_ref.shape[1]
    spectra = near_ref.shape[3]
    half = beams // 2
    data = jnp.concatenate([near_ref[:, 0], far_ref[:, 0]], axis=0).astype(jnp.float32)
    real, imag = data[:, :OWN], data[:, OWN:]
    of_real = jnp.concatenate([real, -imag], axis=1).reshape(-1, spectra)
    of_imag = jnp.concatenate([imag, real], axis=1).reshape(-1, spectra)
    both = jnp.concatenate([of_real, of_imag], axis=1).astype(jnp.bfloat16)
    product = jnp.dot(weights_ref[0], both, preferred_element_type=jnp.float32)
    for part in range(2):
        mine = product[:, part * spectra : (part + 1) * spectra]
        quarter = half // 4
        for block in range(4):
            at = (block % 2, block // 2) if turned else (block // 2, block % 2)
            rows = slice(block * quarter, (block + 1) * quarter)
            keep_ref[at[0], at[1], 0, part] = mine[:half][rows]
            send_ref[at[0], at[1], 0, part] = mine[half:][rows].astype(jnp.bfloat16)


def combine(arranged, near, near_from, far, chunk):
    beams, wide = arranged.shape[1:]
    sources, chans, rows, spectra = far.shape
    shape = (2, 2, chans, 2, beams // 8, spectra)
    block = pl.BlockSpec((2, 2, 1, 2, beams // 8, spectra), lambda c: (0, 0, c, 0, 0, 0))
    return pl.pallas_call(
        functools.partial(combine_kernel, chunk == 1),
        grid=(chans,),
        out_shape=(jax.ShapeDtypeStruct(shape, jnp.float32), jax.ShapeDtypeStruct(shape, jnp.bfloat16)),
        in_specs=[
            pl.BlockSpec((1, beams, wide), lambda c: (c, 0, 0)),
            pl.BlockSpec((sources, 1, rows, spectra), lambda c: (0, near_from + c, 0, 0)),
            pl.BlockSpec((sources, 1, rows, spectra), lambda c: (0, c, 0, 0)),
        ],
        out_specs=(block, block),
        compiler_params=pltpu.CompilerParams(vmem_limit_bytes=SMALL),
        cost_estimate=SHORT,
    )(arranged, near, far)


def fine_tables():
    steps = np.arange(UPCH)
    angles = 2.0 * math.pi * (np.outer(steps, steps) % UPCH) / UPCH
    eye = np.eye(SPECTRA // UPCH)
    real = np.kron(eye, np.cos(angles) / math.sqrt(UPCH))
    imag = np.kron(eye, -np.sin(angles) / math.sqrt(UPCH))
    turn = np.block([[real, imag], [-imag, real]]).astype(np.float32)
    mean = np.tile(np.eye(UPCH) * UPCH / SPECTRA, (1, SPECTRA // UPCH)).astype(np.float32)
    high = turn.astype(jnp.bfloat16)
    low = (turn - high.astype(np.float32)).astype(jnp.bfloat16)
    return np.stack([high, low]), mean


def three_products(value, high, low):
    top = value.astype(jnp.bfloat16)
    rest = (value - top.astype(jnp.float32)).astype(jnp.bfloat16)
    wide = jnp.float32
    total = jnp.dot(top, low, preferred_element_type=wide) + jnp.dot(rest, high, preferred_element_type=wide)
    return total + jnp.dot(top, high, preferred_element_type=wide)


def detect_kernel(*refs):
    halves, (turn_ref, mean_ref, out_ref) = refs[:-3], refs[-3:]
    wide = jnp.float32
    for at in range(0, len(halves), 4):
        keep_ref, come_ref, one_ref, two_ref = halves[at : at + 4]
        total = keep_ref[0, 0] + come_ref[0, 0].astype(wide) + one_ref[0].astype(wide) + two_ref[...].astype(wide)
        chans, _, beams, spectra = total.shape
        both = jnp.concatenate(
            [total[:, 0].reshape(chans * beams, spectra), total[:, 1].reshape(chans * beams, spectra)], axis=1
        )
        sub = three_products(both, turn_ref[0], turn_ref[1])
        power = sub[:, :spectra] * sub[:, :spectra] + sub[:, spectra:] * sub[:, spectra:]
        mean = lax.dot_general(
            mean_ref[...], power, (((1,), (1,)), ((), ())), preferred_element_type=wide, precision=lax.Precision.HIGHEST
        )
        for chan in range(chans):
            out_ref[at // 4 * chans + chan] = mean[:, chan * beams : (chan + 1) * beams]


def detect(halves):
    chans, _, beams, spectra = halves[0][0].shape[2:]
    turn, mean = fine_tables()
    block = (chans, 2, beams, spectra)
    corner = pl.BlockSpec((1, 1) + block, lambda k: (0,) * 6)
    one = pl.BlockSpec((1,) + block, lambda k: (0,) * 5)
    two = pl.BlockSpec(block, lambda k: (0,) * 4)
    whole = pl.BlockSpec(memory_space=pltpu.VMEM)
    return pl.pallas_call(
        detect_kernel,
        grid=(1,),
        out_shape=jax.ShapeDtypeStruct((len(halves) * chans, UPCH, beams), jnp.float32),
        in_specs=[corner, corner, one, two] * len(halves) + [whole] * 2,
        out_specs=whole,
        compiler_params=pltpu.CompilerParams(vmem_limit_bytes=SMALL),
        cost_estimate=SHORT,
    )(*[part for half in halves for part in half], jnp.asarray(turn), jnp.asarray(mean))


def swap(value, axis, distance, size):
    return lax.ppermute(value, axis, [(k, k ^ distance) for k in range(size)])


def after(value, earlier):
    return lax.optimization_barrier((value, earlier))[0]


def narrow(value):
    return value.astype(jnp.bfloat16)


def widen(value):
    return value.astype(jnp.float32)


def channel_table(chans):
    rows = transform_table().reshape(4, 2, 4, 2, chans, NFFT)
    return jnp.asarray(np.transpose(rows, (1, 3, 0, 2, 4, 5)).reshape(2, 2, 16 * chans, NFFT))


def on_device(voltages, weights, input_map, beam_order):
    chans = weights.shape[0]
    half = chans // 2
    table = channel_table(chans)
    z_hi = lax.axis_index("zh")
    y, x = lax.axis_index("y"), lax.axis_index("x")
    core, z = lax.axis_index("core"), lax.axis_index("zl")
    where = jnp.stack([z_hi, 4 * y + x, core, z]).astype(jnp.int32)

    def turn_by_swaps(value):
        value = value.reshape(4, 4, -1, SPECTRA)
        rows = [value[0]] + [swap(value[k], "y", k, 4) for k in (1, 2, 3)]
        columns = [jnp.stack([row[k] for row in rows]) for k in range(4)]
        columns = [columns[0]] + [swap(columns[k], "x", k, 4) for k in (1, 2, 3)]
        return jnp.stack(columns).reshape(PLANE, -1, 2 * OWN, SPECTRA)

    def turn(value):
        value = lax.all_to_all(value.reshape(PLANE, -1, SPECTRA), ("y", "x"), split_axis=0, concat_axis=0, tiled=True)
        return value.reshape(PLANE, -1, 2 * OWN, SPECTRA)

    first, rest = channelize(voltages, table)
    far0 = swap(first, "zh", 1, 2)
    planed = turn(rest)
    far1 = swap(planed[:, :half], "zh", 1, 2)
    arranged0 = arrange_weights(where, after(weights, rest), beam_order, input_map, 0)
    arranged1 = arrange_weights(where, after(weights, arranged0), beam_order, input_map, 1)
    data0 = after(turn_by_swaps(after(after(far0, arranged1), planed)), far1)

    keep0, send0 = combine(arranged0, planed, half, data0, 0)
    come0 = swap(send0, "core", 1, 2)
    to0 = narrow(keep0[1] + widen(come0[1]))
    keep1, send1 = combine(arranged1, planed, 2 * half, far1, 1)
    come1 = swap(send1, "core", 1, 2)
    one0 = swap(to0, "zl", 2, 4)
    one1 = swap(narrow(keep1[1] + widen(come1[1])), "zl", 1, 4)
    two0 = swap(narrow(keep0[0, 1] + widen(come0[0, 1]) + widen(one0[1])), "zl", 1, 4)
    two1 = swap(narrow(keep1[0, 1] + widen(come1[0, 1]) + widen(one1[1])), "zl", 2, 4)
    return detect([(keep0, come0, one0, two0), (keep1, come1, one1, two1)])


def solution(mesh):
    fine = Mesh(mesh.devices.reshape(4, 2, 4, 2, 4), ("zl", "core", "y", "zh", "x"))
    grp, dev = ("zl", "core"), ("y", "zh", "x")
    placed = (P(grp + dev, None), P(dev, None, None, grp), P(grp), P())
    return jax.shard_map(on_device, mesh=fine, in_specs=placed, out_specs=P(dev, None, grp), check_vma=False)
```
